32 devices in a mesh: dp: 4 (over z), worker: 8 (over y, x, core).
Axes of the slice: x: 2, y: 2, z: 4, core: 2. Of those that a mesh axis runs over, the one named last changes fastest.
Arguments:
- grads: bfloat16 [4, 8, 1024, 1024], P('dp', 'worker')
- owner_slots: int32 [8, 3], replicated, may hold values from 0 to 7, as said below
- owner_counts: int32 [8], replicated, may hold values from 0 to 3, as said below
- stat_left: float32 [8, 3, 1024, 1024], P('worker', None, 'dp'), may hold values from -6 to 6
- stat_right: float32 [8, 3, 1024, 1024], P('worker', None, 'dp'), may hold values from -6 to 6
- inv_left: float32 [8, 3, 1024, 1024], P('worker', None, 'dp')
- inv_right: float32 [8, 3, 1024, 1024], P('worker', None, 'dp')
Outputs:
- new_left: float32 [8, 3, 1024, 1024], P('worker', None, 'dp')
- new_right: float32 [8, 3, 1024, 1024], P('worker', None, 'dp')
- directions: bfloat16 [8, 3, 1024, 1024], P('worker')
The draws below stay inside these ranges and needn't reach their ends.
Inputs may be any that keep to these rules, and one draw needn't show every extreme that they name: `owner_slots`: for each owner o the entries s < owner_counts[o] name blocks, and over all owners these name each of the 8 blocks exactly once; the other entries are arbitrary block numbers. `owner_counts`: the counts sum to 8.
All inputs are finite; a program needn't handle non-finite values.
Results may differ from the reference program's by a relative error of at most 0.012.
Values may be sent and summed in bfloat16 or wider, within the bound.
No kernel may reach another device: no remote copies, remote signals or barrier semaphores. Data moves between devices by JAX's collectives and lax.ppermute only.
A program may use at most 128 MiB of HBM per device.

```python
import math
import jax
import jax.numpy as jnp
from jax import lax

BLK = 1024
CAP = 3
NB = 8
N_DP = 4
N_WORKER = 8


def assignment(key):
    key = jax.random.fold_in(key, 11)
    key_full, key_seat, key_block, key_filler = jax.random.split(key, 4)
    seat_total = N_WORKER * CAP
    full_owner = jax.random.randint(key_full, (), 0, N_WORKER)
    seat_owner = jnp.arange(seat_total) // CAP
    priority = jax.random.permutation(key_seat, seat_total)
    score = priority + seat_total * (seat_owner != full_owner).astype(jnp.int32)
    order = jnp.argsort(score, stable=True)
    chosen = jnp.zeros((seat_total,), jnp.int32).at[order[:NB]].set(1)
    counts = jnp.sum(chosen.reshape(N_WORKER, CAP), axis=1)
    offsets = jnp.cumsum(counts) - counts
    block_order = jax.random.permutation(key_block, NB)
    slot_index = jnp.arange(CAP)[None, :]
    position = jnp.clip(offsets[:, None] + slot_index, 0, NB - 1)
    filler = jax.random.randint(key_filler, (N_WORKER, CAP), 0, NB)
    table = jnp.where(slot_index < counts[:, None], block_order[position], filler)
    return (table.astype(jnp.int32), counts.astype(jnp.int32))


def draw_owner_slots(key, part):
    table, counts = assignment(key)
    return table


def draw_owner_counts(key, part):
    table, counts = assignment(key)
    return counts


def draw_grads(key, part):
    key = jax.random.fold_in(key, 5)
    key_row, key_col, key_own = jax.random.split(key, 3)
    position = jnp.arange(BLK, dtype=jnp.float32) / BLK
    row_scale = jnp.exp(math.log(10.0) * (position - 0.5)) * jnp.exp(jax.random.uniform(key_row, (BLK,), jnp.float32, 0.0, math.log(1.5)))
    col_scale = jnp.exp(jax.random.uniform(key_col, (BLK,), jnp.float32, math.log(0.3), math.log(3.0)))
    values = jax.random.normal(key_own, (N_DP, NB, BLK, BLK), jnp.float32)
    return (values * row_scale[:, None] * col_scale[None, :]).astype(jnp.bfloat16)


def root_matrix(key, spread):
    key_off, key_diag = jax.random.split(key)
    noise = jax.random.normal(key_off, (N_WORKER, CAP, BLK, BLK), jnp.float32)
    symmetric = (noise + jnp.swapaxes(noise, 2, 3)) * (0.5 / math.sqrt(BLK))
    diagonal = jnp.exp(jax.random.uniform(key_diag, (N_WORKER, CAP, BLK), jnp.float32, -spread, spread))
    return symmetric + diagonal[:, :, :, None] * jnp.eye(BLK, dtype=jnp.float32)


def draw_inv_left(key, part):
    key = jax.random.fold_in(key, 21)
    return root_matrix(key, 0.7)


def draw_inv_right(key, part):
    key = jax.random.fold_in(key, 31)
    return root_matrix(key, 0.7)


def level_of(stream_key, shape, cuts, smallest, largest):
    factor_of = 1.0
    for axis_at, blocks in cuts:
        steps = jax.random.uniform(jax.random.fold_in(jax.random.fold_in(stream_key, 6), axis_at), (blocks,), jnp.float32, smallest / len(cuts), largest / len(cuts))
        factor_of = factor_of * jnp.repeat(jnp.exp(steps), shape[axis_at] // blocks).reshape((-1,) + (1,) * (len(shape) - 1 - axis_at))
    return factor_of


def bell_draw(own_key, dims, scale, reach, shards=(), kind=jnp.bfloat16):
    level = level_of(own_key, dims, shards, -0.22, 0.18) if shards else 1.0
    array = jax.random.normal(own_key, dims, jnp.float32) * scale * level
    return jnp.minimum(jnp.maximum(array, -reach), reach).astype(kind)


def setup_inputs(seed: int = 0) -> dict:
    splits = jax.random.split(jax.random.key(seed), 8)
    return {
        "grads": draw_grads(jax.random.fold_in(splits[7], 71), 0),
        "owner_slots": draw_owner_slots(jax.random.fold_in(splits[7], 71), 0),
        "owner_counts": draw_owner_counts(jax.random.fold_in(splits[7], 71), 0),
        "stat_left": bell_draw(splits[3], (N_WORKER, CAP, BLK, BLK), 1.0, 6.0, ((0, 8), (2, 4)), jnp.float32),
        "stat_right": bell_draw(splits[4], (N_WORKER, CAP, BLK, BLK), 1.0, 6.0, ((0, 8), (2, 4)), jnp.float32),
        "inv_left": draw_inv_left(jax.random.fold_in(splits[7], 71), 0),
        "inv_right": draw_inv_right(jax.random.fold_in(splits[7], 71), 0),
    }


STAT_DECAY = 0.9
EPSILON = 1e-06

def reference(grads, owner_slots, owner_counts, stat_left, stat_right, inv_left, inv_right):
    highest = lax.Precision.HIGHEST
    grad_mean = lax.optimization_barrier(jnp.mean(grads.astype(jnp.float32), axis=0))
    live_mask = (jnp.arange(CAP)[None, :] < owner_counts[:, None]).astype(jnp.float32)
    slot_grad = grad_mean[owner_slots] * live_mask[:, :, None, None]
    update_scale = (1.0 - STAT_DECAY) / BLK
    left_update = jnp.einsum('osik,osjk->osij', slot_grad, slot_grad, precision=highest)
    right_update = jnp.einsum('osji,osjk->osik', slot_grad, slot_grad, precision=highest)
    new_left = STAT_DECAY * stat_left + update_scale * left_update
    new_right = STAT_DECAY * stat_right + update_scale * right_update
    left_part = jnp.einsum('osij,osjk->osik', inv_left, slot_grad, precision=highest)
    raw_dir = jnp.einsum('osij,osjk->osik', left_part, inv_right, precision=highest)
    grad_square = lax.optimization_barrier(jnp.sum(slot_grad * slot_grad, axis=(2, 3)))
    raw_square = lax.optimization_barrier(jnp.sum(raw_dir * raw_dir, axis=(2, 3)))
    graft_ratio = jnp.sqrt((grad_square + EPSILON) / (raw_square + EPSILON))
    directions = (raw_dir * graft_ratio[:, :, None, None]).astype(jnp.bfloat16)
    return (new_left, new_right, directions)
```

```python
import functools
import jax
import jax.numpy as jnp
from jax import lax
from jax.experimental import pallas as pl
from jax.experimental.pallas import tpu as pltpu
from jax.sharding import PartitionSpec as P

STAT_DECAY = 0.9
EPSILON = 1e-06
BF = jnp.bfloat16
F32 = jnp.float32
ANY = pl.BlockSpec(memory_space=pl.ANY)
SMEM = pl.BlockSpec(memory_space=pltpu.SMEM)
VMEM_LIMIT = 56 * 1024 * 1024

LEVEL, CORE, ZPOS, XSHIP, YSHIP, XIN, YIN = range(7)
SEAT = 8
LIVE = 16
BLOCK = 20
CAND = 24
MATE = 28
UNIT = 32
PLAN = 40


def plan_kernel(spill, cap, cols, where_ref, slots_ref, counts_ref, out_ref):
    z, w = where_ref[0], where_ref[1]
    core, col = lax.rem(w, 2), lax.div(w, 2)
    per = lambda c: counts_ref[2 * c] + counts_ref[2 * c + 1]
    per_col = [counts_ref[2 * c] + counts_ref[2 * c + 1] for c in range(cols)]
    if spill:
        combo = lax.broadcasted_iota(jnp.int32, (8, 128), 0) * 128 + lax.broadcasted_iota(jnp.int32, (8, 128), 1)
        combo = combo & 255
        bit = [(combo >> k) & 1 for k in range(8)]
        worst = jnp.zeros((8, 128), jnp.int32)
        bad = jnp.zeros((8, 128), jnp.int32)
        ships = jnp.zeros((8, 128), jnp.int32)
        for c in range(4):
            out = bit[c] + bit[4 + c]
            load = per_col[c] - out + bit[c ^ 1] + bit[4 + (c ^ 2)]
            worst = jnp.maximum(worst, load)
            bad = jnp.maximum(bad, jnp.where(out > per_col[c], 1, 0))
            ships = ships + out
        cost = (worst * 16 + ships + bad * 1024) * 256 + combo
        best = jnp.min(cost.astype(F32)).astype(jnp.int32)
        level = lax.div(best, 4096)
        flows = best & 255
        flag = lambda k: (flows >> k) & 1
        xship, yship = flag(col), flag(4 + col)
        xin, yin = flag(col ^ 1), flag(4 + (col ^ 2))
    else:
        level = functools.reduce(jnp.maximum, per_col)
        xship = yship = xin = yin = jnp.int32(0)
    if spill:
        x_rank = per(col ^ 1) - 1
        y_rank = per(col ^ 2) - 1 - flag(col ^ 2)
    first = counts_ref[2 * col]
    mine = counts_ref[2 * col + 1] + first

    def seat(rank):
        c = jnp.where(rank < first, 0, 1)
        s = jnp.minimum(jnp.maximum(rank - c * first, 0), cap - 1)
        return jnp.where(c == core, 0, cap) + s

    def block_at(column, rank):
        start = counts_ref[2 * column]
        c = jnp.where(rank < start, 0, 1)
        return slots_ref[2 * column + c, jnp.minimum(jnp.maximum(rank - c * start, 0), cap - 1)] ^ w

    out_ref[LEVEL] = level
    out_ref[CORE] = core
    out_ref[ZPOS] = z
    out_ref[XIN] = xin
    out_ref[YIN] = yin
    out_ref[XSHIP] = seat(mine - 1)
    out_ref[YSHIP] = seat(mine - 1 - xship)
    for i in range(2 * cap):
        rank = 0 if i == 0 else (1 - xin if i == 1 else i - xin - yin)
        out_ref[SEAT + i] = seat(jnp.int32(rank))
        block = block_at(col, jnp.int32(rank))
        if spill and i == 0:
            block = jnp.where(xin == 1, block_at(col ^ 1, x_rank), block)
        if spill and i == 1:
            block = jnp.where(yin == 1, block_at(col ^ 2, y_rank), block)
        out_ref[UNIT + i] = block
    for s in range(cap):
        rank = s + core * first
        out_ref[LIVE + s] = jnp.where(s < counts_ref[w], 1, 0)
        out_ref[BLOCK + s] = slots_ref[w, s] ^ w
        out_ref[MATE + s] = slots_ref[w ^ 1, s] ^ w
        place = jnp.where(xin + yin == 0, rank, jnp.where(xin == 0, jnp.where(rank == 0, 0, rank + 1), rank + xin + yin))
        sent_x = jnp.logical_and(xship == 1, rank == mine - 1)
        sent_y = jnp.logical_and(yship == 1, rank == mine - 1 - xship)
        out_ref[CAND + s] = jnp.where(sent_x, 100, jnp.where(sent_y, 101, place))


def pick(plan, picks, sources, rows, cols_, out_counts):
    n_src = len(sources)

    def kernel(plan_ref, *refs):
        src, outs, sem = refs[:n_src], refs[n_src:-1], refs[-1]
        flat = [(o, k) for o, count in enumerate(out_counts) for k in range(count)]
        for at, ((o, k), options) in enumerate(zip(flat, picks, strict=True)):
            for condition, which, index in options:

                def start(which=which, index=index, o=o, k=k, at=at):
                    pltpu.make_async_copy(src[which].at[index(plan_ref)], outs[o].at[k], sem.at[at]).start()

                pl.when(condition(plan_ref))(start)
        for at, (o, k) in enumerate(flat):
            pltpu.make_async_copy(outs[o].at[k], outs[o].at[k], sem.at[at]).wait()

    return pl.pallas_call(
        kernel,
        out_shape=[jax.ShapeDtypeStruct((count, rows, cols_), BF) for count in out_counts],
        in_specs=[SMEM] + [ANY] * n_src,
        out_specs=[pl.BlockSpec(memory_space=pltpu.VMEM)] * len(out_counts),
        scratch_shapes=[pltpu.SemaphoreType.DMA((len(picks),))],
        compiler_params=pltpu.CompilerParams(vmem_limit_bytes=VMEM_LIMIT),
        name="pick",
    )(plan, *sources)


def stat_kernel(size, cap, cands, n_pieces, plan_ref, ours_ref, theirs_ref, *refs):
    pieces = refs[:n_pieces]
    left_ref, right_ref, new_left_ref, new_right_ref, full_ref, held, sem = refs[n_pieces:]
    step = pl.program_id(0)
    z, core = plan_ref[ZPOS], plan_ref[CORE]
    block, cols = held.shape[1:]
    rows = block // size
    half = rows // 2

    def fetch(s):
        def copy(source, shard, side):
            row = pl.multiple_of(shard * rows + side * half, 16)
            pltpu.make_async_copy(source, held.at[s, pl.ds(row, half), :], sem.at[s]).start()

        @pl.when(plan_ref[LIVE + s] == 1)
        def _():
            copy(ours_ref.at[s], z, core)
            copy(theirs_ref.at[s], z, 1 - core)

        for number, local, partner in cands:

            @pl.when(jnp.logical_and(plan_ref[LIVE + s] == 1, plan_ref[CAND + s] == number))
            def _():
                for chosen, side in ((local, core), (partner, 1 - core)):
                    for ref, index, offset in chosen:
                        copy(pieces[ref].at[index], lax.rem(z + offset, size), side)

    @pl.when(step == 0)
    def _():
        for s in range(cap):
            fetch(s)

    live = plan_ref[LIVE + step] == 1
    scale = (1.0 - STAT_DECAY) / cols

    @pl.when(live)
    def _():
        pltpu.make_async_copy(held.at[step], held.at[step], sem.at[step]).wait()
        g = held[step]
        start = pl.multiple_of(z * rows, 128)
        g_rows = held[step, pl.ds(start, rows), :]
        g_cols = held[step, :, pl.ds(start, rows)]
        left = lax.dot_general(g_rows, g, (((1,), (1,)), ((), ())), preferred_element_type=F32)
        new_left_ref[0] = STAT_DECAY * left_ref[0] + scale * left
        right = lax.dot_general(g_cols, g, (((0,), (0,)), ((), ())), preferred_element_type=F32)
        new_right_ref[0] = STAT_DECAY * right_ref[0] + scale * right
        full_ref[0] = g

    @pl.when(jnp.logical_not(live))
    def _():
        new_left_ref[0] = STAT_DECAY * left_ref[0]
        new_right_ref[0] = STAT_DECAY * right_ref[0]
        full_ref[0] = jnp.zeros_like(full_ref[0])


def direction_kernel(size, cap, cands, n_pieces, returned, plan_ref, full_ref, mine_ref, other_ref, *refs):
    pieces = refs[:n_pieces]
    out_ref, left, right, grad, raw, made_out, sem, out_sem = refs[n_pieces + returned :]
    step = pl.program_id(0)
    z, core = plan_ref[ZPOS], plan_ref[CORE]
    block = raw.shape[0]
    rows = block // size

    def live(s):
        return plan_ref[LIVE + s] == 1

    def active(s):
        came_back = plan_ref[CAND + s] >= 100
        return jnp.logical_and(live(s), came_back if returned else jnp.logical_not(came_back))

    def fetch(s):
        @pl.when(active(s))
        def _():
            pltpu.make_async_copy(full_ref.at[s], grad.at[s], sem.at[s, 2]).start()

        for kind, held in ((0, left), (1, right)):
            for here in (True, False):
                side = core == kind if here else core != kind
                use = jnp.logical_and(active(s), side)
                own = mine_ref if here else other_ref

                def start_own(own=own, held=held, kind=kind):
                    row = pl.multiple_of(z * rows, 16)
                    pltpu.make_async_copy(own.at[s], held.at[s, pl.ds(row, rows), :], sem.at[s, kind]).start()

                pl.when(use)(start_own)
                for number, local, partner in cands:

                    def start(chosen=local if here else partner, held=held, kind=kind):
                        for ref, index, offset in chosen:
                            row = pl.multiple_of(lax.rem(z + offset, size) * rows, 16)
                            target = held.at[s, pl.ds(row, rows), :]
                            pltpu.make_async_copy(pieces[ref].at[index], target, sem.at[s, kind]).start()

                    pl.when(jnp.logical_and(use, plan_ref[CAND + s] == number))(start)

    @pl.when(step == 0)
    def _():
        for s in range(cap):
            fetch(s)

    @pl.when(active(step))
    def _():
        for kind, held in ((0, left), (1, right), (2, grad)):
            pltpu.make_async_copy(held.at[step], held.at[step], sem.at[step, kind]).wait()
        g_square = jnp.zeros((8, block), F32)
        raw_square = jnp.zeros((8, block), F32)
        tile = 256
        for r in range(0, block, tile):
            part = jnp.dot(left[step, r : r + tile, :], grad[step], preferred_element_type=F32).astype(BF)
            made = jnp.dot(part, right[step], preferred_element_type=F32)
            raw[r : r + tile, :] = made
            raw_square += jnp.sum((made * made).reshape(tile // 8, 8, block), axis=0)
            g = grad[step, r : r + tile, :].astype(F32)
            g_square += jnp.sum((g * g).reshape(tile // 8, 8, block), axis=0)
        top = jnp.sum(g_square, axis=(0, 1), keepdims=True) + EPSILON
        bottom = jnp.sum(raw_square, axis=(0, 1), keepdims=True) + EPSILON
        graft = jnp.sqrt(top / bottom)
        made_out[step] = (raw[...] * graft).astype(BF)
        pltpu.make_async_copy(made_out.at[step], out_ref.at[step], out_sem.at[step]).start()

    if not returned:

        @pl.when(jnp.logical_not(live(step)))
        def _():
            made_out[step] = jnp.zeros_like(made_out[step])
            pltpu.make_async_copy(made_out.at[step], out_ref.at[step], out_sem.at[step]).start()

    @pl.when(step == cap - 1)
    def _():
        for s in range(cap):
            written = active(s) if returned else jnp.logical_or(active(s), jnp.logical_not(live(s)))

            @pl.when(written)
            def _():
                pltpu.make_async_copy(made_out.at[s], out_ref.at[s], out_sem.at[s]).wait()


def step_at(level, spill, plan, core, grads, stat_left, stat_right, inv_left, inv_right):
    size, workers = lax.axis_size("dp"), lax.axis_size("worker")
    z = lax.axis_index("dp")
    cap, rows, cols = inv_left.shape
    block, part = rows * size, rows // 2
    up_pairs = [(i, i + 1) for i in range(size - 1)]
    down_pairs = [(i + 1, i) for i in range(size - 1)]
    around = [(i, (i + 1) % size) for i in range(size)]
    ring = lambda x: lax.ppermute(x, "dp", around)
    across = lambda x, k: lax.ppermute(x, "worker", [(i, i ^ k) for i in range(workers)])

    def after(given, *xs):
        xs = lax.optimization_barrier((*xs, *given))[: len(xs)]
        return xs if len(xs) > 1 else xs[0]

    numbers = list(range(level)) + ([100, 101] if spill else [])

    def bring(cands, arrays, t, moved):
        found = [(moved, u) for u in range(level)]
        if len(cands) > level:
            found += [(across(moved[0:1], 2), 0), (across(moved[1:2], 4), 0)]
        twins = {}
        for (_, local, partner), (array, index) in zip(cands, found, strict=True):
            if id(array) not in twins:
                twins[id(array)] = len(arrays)
                arrays.extend([array, across(array, 1)])
            at = twins[id(array)]
            local.append((at, index, size - t))
            partner.append((at + 1, index, size - t))

    g = grads.reshape(size, rows, cols)

    def sum_step(t, up, down):
        send_up = lax.dynamic_index_in_dim(g, jnp.minimum(size - t + z, size - 1), 0, keepdims=False)
        send_down = lax.dynamic_index_in_dim(g, jnp.maximum(z - size + t, 0), 0, keepdims=False)
        if t > 1:
            send_up = (send_up.astype(F32) + up.astype(F32)).astype(BF)
            send_down = (send_down.astype(F32) + down.astype(F32)).astype(BF)
        return send_up, send_down

    def sum_send(t, send_up, send_down):
        return lax.ppermute(send_up, "dp", up_pairs[:t]), lax.ppermute(send_down, "dp", down_pairs[size - 1 - t :])

    sends = sum_step(1, None, None)
    up, down = sum_send(1, *sends)
    inv_left, inv_right = after(sends, inv_left, inv_right)

    left_b, right_b = inv_left.astype(BF), inv_right.astype(BF)
    mine = jnp.where(core == 0, left_b, right_b)
    other = jnp.where(core == 0, right_b, left_b)
    theirs = across(other, 1)
    seat_of = lambda at: [
        (lambda plan_ref: plan_ref[at] < cap, 0, lambda plan_ref: plan_ref[at]),
        (lambda plan_ref: plan_ref[at] >= cap, 1, lambda plan_ref: plan_ref[at] - cap),
    ]
    sources = [mine, theirs]
    picks = [seat_of(SEAT + i) for i in range(level)]
    if spill:
        out_x, out_y = pick(plan, [seat_of(XSHIP), seat_of(YSHIP)], sources, rows, cols, (1, 1))
        sources += [across(out_x, 2), across(out_y, 4)]
        for i, flag in ((0, XIN), (1, YIN)):
            own_options = [
                (lambda plan_ref, c=c, flag=flag: jnp.logical_and(c(plan_ref), plan_ref[flag] == 0), which, index)
                for c, which, index in picks[i]
            ]
            picks[i] = own_options + [(lambda plan_ref, flag=flag: plan_ref[flag] == 1, 2 + i, lambda plan_ref: 0)]
        up, down = after((out_x, out_y), up, down)
    (units,) = pick(plan, picks, sources, rows, cols, (level,))
    root = [ring(units)]
    for t in range(2, size):
        sends = sum_step(t, up, down)
        up, down = sum_send(t, *sends)
        if t == 2:
            up, down = after((units,), up, down)
    own = lax.dynamic_index_in_dim(g, z, 0, keepdims=False).astype(F32)
    own = ((own + up.astype(F32) + down.astype(F32)) / size).astype(BF)

    halves = own.reshape(2, part, cols)
    keep = lax.dynamic_index_in_dim(halves, core, 0, keepdims=False)
    give = lax.dynamic_index_in_dim(halves, 1 - core, 0, keepdims=False)
    home = jnp.stack([keep, across(give, 1)])
    n_bits = workers.bit_length() - 1
    if n_bits == 3:
        from_x, from_y = across(home, 2), across(home, 4)
        corner = [across(from_x[0:1], 4), across(from_y[1:2], 2)]
        spread = [home, from_x, from_y, *corner]
        where_is = [(0, 0), (0, 1), (1, 0), (1, 1), (2, 0), (2, 1), (3, 0), (4, 0)]
    else:
        spread = [home]
        for b in range(1, n_bits):
            spread += [across(array, 1 << b) for array in spread]
        where_is = [(j >> 1, j & 1) for j in range(workers)]
    block_of = lambda at: [
        (lambda plan_ref, j=j: plan_ref[at] == j, which, lambda plan_ref, index=index: index)
        for j, (which, index) in enumerate(where_is)
    ]
    wanted = [block_of(UNIT + i) for i in range(level)]
    wanted += [block_of(BLOCK + s) for s in range(cap)] + [block_of(MATE + s) for s in range(cap)]
    g_units, g_ours, g_mates = pick(plan, wanted, spread, part, cols, (level, cap, cap))
    g_theirs = across(g_mates, 1)

    arrays, cands = [], [(number, [], []) for number in numbers]
    g_arrays, g_cands = [], [(number, [], []) for number in numbers]
    root.append(ring(root[0]))
    g_moved = after((root[1],), g_units)
    for t in range(1, size):
        before = g_moved
        g_moved = ring(before)
        bring(g_cands, g_arrays, t, g_moved)
        if t < size - 1:
            if t > 1:
                root.append(ring(after((before,), root[t - 1])))
            start = len(arrays)
            bring(cands, arrays, t, root[t - 1])
            g_moved = after(arrays[start:], g_moved)

    slot = lambda r: pl.BlockSpec((1, r, cols), lambda s: (s, 0, 0))
    new_left, new_right, full = pl.pallas_call(
        functools.partial(stat_kernel, size, cap, g_cands, len(g_arrays)),
        grid=(cap,),
        out_shape=[
            jax.ShapeDtypeStruct((cap, rows, cols), F32),
            jax.ShapeDtypeStruct((cap, rows, cols), F32),
            jax.ShapeDtypeStruct((cap, block, cols), BF),
        ],
        in_specs=[SMEM] + [ANY] * (2 + len(g_arrays)) + [slot(rows), slot(rows)],
        out_specs=[slot(rows), slot(rows), slot(block)],
        scratch_shapes=[pltpu.VMEM((cap, block, cols), BF), pltpu.SemaphoreType.DMA((cap,))],
        compiler_params=pltpu.CompilerParams(vmem_limit_bytes=VMEM_LIMIT),
        name="statistics",
    )(plan, g_ours, g_theirs, *g_arrays, stat_left, stat_right)

    final = after((new_left, new_right), root[-1])
    back = [across(final[0:1], 2), across(final[1:2], 4)] if spill else []
    bring(cands[:level], arrays, size - 1, final)

    def direct(chosen, before):
        used = sorted({ref for _, local, partner in chosen for ref, _, _ in local + partner})
        renamed = [
            (number, *([(used.index(ref), index, offset) for ref, index, offset in refs] for refs in (local, partner)))
            for number, local, partner in chosen
        ]
        return pl.pallas_call(
            functools.partial(direction_kernel, size, cap, renamed, len(used), len(before)),
            grid=(cap,),
            out_shape=jax.ShapeDtypeStruct((cap, block, cols), BF),
            in_specs=[SMEM] + [ANY] * (3 + len(used) + len(before)),
            out_specs=ANY,
            input_output_aliases={4 + len(used): 0} if before else {},
            scratch_shapes=[pltpu.VMEM((cap, block, cols), BF) for _ in range(3)]
            + [pltpu.VMEM((block, cols), F32), pltpu.VMEM((cap, block, cols), BF)]
            + [pltpu.SemaphoreType.DMA((cap, 3)), pltpu.SemaphoreType.DMA((cap,))],
            compiler_params=pltpu.CompilerParams(vmem_limit_bytes=VMEM_LIMIT),
            name="direction",
        )(plan, full, mine, other, *(arrays[ref] for ref in used), *before)

    directions = direct(cands[:level], [])
    if spill:
        back = after((directions,), *back)
        for cand, array in zip(cands[level:], back, strict=True):
            for refs, ref in ((cand[1], array), (cand[2], across(array, 1))):
                refs.append((len(arrays), 0, 1))
                arrays.append(ref)
        directions = direct(cands[level:], [directions])
    return new_left, new_right, directions


def on_device(grads, owner_slots, owner_counts, stat_left, stat_right, inv_left, inv_right):
    workers = lax.axis_size("worker")
    cap = owner_slots.shape[1]
    cols = workers // 2
    spill = cols == 4
    where = jnp.stack([lax.axis_index("dp"), lax.axis_index("worker")]).astype(jnp.int32)
    plan = pl.pallas_call(
        functools.partial(plan_kernel, spill, cap, cols),
        out_shape=jax.ShapeDtypeStruct((PLAN,), jnp.int32),
        in_specs=[SMEM] * 3,
        out_specs=SMEM,
        name="plan",
    )(where, owner_slots, owner_counts)
    core = lax.axis_index("worker") % 2
    levels = range(2, 5) if spill else [2 * cap]
    branches = [functools.partial(step_at, level, spill) for level in levels]
    operands = (plan, core, grads[0, 0], stat_left[0], stat_right[0], inv_left[0], inv_right[0])
    if spill:
        outs = lax.switch(plan[LEVEL] - levels[0], branches, *operands)
    else:
        outs = branches[0](*operands)
    return tuple(out[None] for out in outs)


def solution(mesh):
    return jax.shard_map(
        on_device,
        mesh=mesh,
        in_specs=(
            P("dp", "worker", None, None),
            P(),
            P(),
            P("worker", None, "dp", None),
            P("worker", None, "dp", None),
            P("worker", None, "dp", None),
            P("worker", None, "dp", None),
        ),
        out_specs=(
            P("worker", None, "dp", None),
            P("worker", None, "dp", None),
            P("worker", None, None, None),
        ),
        check_vma=False,
    )
```

```python
import functools
import jax
import jax.numpy as jnp
from jax import lax
from jax.experimental import pallas as pl
from jax.experimental.pallas import tpu as pltpu
from jax.sharding import PartitionSpec as P

STAT_DECAY = 0.9
EPSILON = 1e-06
BF = jnp.bfloat16
F32 = jnp.float32
ANY = pl.BlockSpec(memory_space=pl.ANY)
SMEM = pl.BlockSpec(memory_space=pltpu.SMEM)
VMEM_LIMIT = 56 * 1024 * 1024

LEVEL, CORE, ZPOS, XSHIP, YSHIP, XIN, YIN = range(7)
SEAT = 8
LIVE = 16
BLOCK = 20
CAND = 24
MATE = 28
UNIT = 32
PLAN = 40


def plan_kernel(spill, cap, cols, where_ref, slots_ref, counts_ref, out_ref):
    z, w = where_ref[0], where_ref[1]
    core, col = lax.rem(w, 2), lax.div(w, 2)
    per = lambda c: counts_ref[2 * c] + counts_ref[2 * c + 1]
    per_col = [counts_ref[2 * c] + counts_ref[2 * c + 1] for c in range(cols)]
    if spill:
        combo = lax.broadcasted_iota(jnp.int32, (8, 128), 0) * 128 + lax.broadcasted_iota(jnp.int32, (8, 128), 1)
        combo = combo & 255
        bit = [(combo >> k) & 1 for k in range(8)]
        worst = jnp.zeros((8, 128), jnp.int32)
        bad = jnp.zeros((8, 128), jnp.int32)
        ships = jnp.zeros((8, 128), jnp.int32)
        for c in range(4):
            out = bit[c] + bit[4 + c]
            load = per_col[c] - out + bit[c ^ 1] + bit[4 + (c ^ 2)]
            worst = jnp.maximum(worst, load)
            bad = jnp.maximum(bad, jnp.where(out > per_col[c], 1, 0))
            ships = ships + out
        cost = (worst * 16 + ships + bad * 1024) * 256 + combo
        best = jnp.min(cost.astype(F32)).astype(jnp.int32)
        level = lax.div(best, 4096)
        flows = best & 255
        flag = lambda k: (flows >> k) & 1
        xship, yship = flag(col), flag(4 + col)
        xin, yin = flag(col ^ 1), flag(4 + (col ^ 2))
    else:
        level = functools.reduce(jnp.maximum, per_col)
        xship = yship = xin = yin = jnp.int32(0)
    if spill:
        x_rank = per(col ^ 1) - 1
        y_rank = per(col ^ 2) - 1 - flag(col ^ 2)
    first = counts_ref[2 * col]
    mine = counts_ref[2 * col + 1] + first

    def seat(rank):
        c = jnp.where(rank < first, 0, 1)
        s = jnp.minimum(jnp.maximum(rank - c * first, 0), cap - 1)
        return jnp.where(c == core, 0, cap) + s

    def block_at(column, rank):
        start = counts_ref[2 * column]
        c = jnp.where(rank < start, 0, 1)
        return slots_ref[2 * column + c, jnp.minimum(jnp.maximum(rank - c * start, 0), cap - 1)] ^ w

    out_ref[LEVEL] = level
    out_ref[CORE] = core
    out_ref[ZPOS] = z
    out_ref[XIN] = xin
    out_ref[YIN] = yin
    out_ref[XSHIP] = seat(mine - 1)
    out_ref[YSHIP] = seat(mine - 1 - xship)
    for i in range(2 * cap):
        rank = 0 if i == 0 else (1 - xin if i == 1 else i - xin - yin)
        out_ref[SEAT + i] = seat(jnp.int32(rank))
        block = block_at(col, jnp.int32(rank))
        if spill and i == 0:
            block = jnp.where(xin == 1, block_at(col ^ 1, x_rank), block)
        if spill and i == 1:
            block = jnp.where(yin == 1, block_at(col ^ 2, y_rank), block)
        out_ref[UNIT + i] = block
    for s in range(cap):
        rank = s + core * first
        out_ref[LIVE + s] = jnp.where(s < counts_ref[w], 1, 0)
        out_ref[BLOCK + s] = slots_ref[w, s] ^ w
        out_ref[MATE + s] = slots_ref[w ^ 1, s] ^ w
        place = jnp.where(xin + yin == 0, rank, jnp.where(xin == 0, jnp.where(rank == 0, 0, rank + 1), rank + xin + yin))
        sent_x = jnp.logical_and(xship == 1, rank == mine - 1)
        sent_y = jnp.logical_and(yship == 1, rank == mine - 1 - xship)
        out_ref[CAND + s] = jnp.where(sent_x, 100, jnp.where(sent_y, 101, place))


def pick(plan, picks, sources, rows, cols_, out_counts):
    n_src = len(sources)

    def kernel(plan_ref, *refs):
        src, outs, sem = refs[:n_src], refs[n_src:-1], refs[-1]
        flat = [(o, k) for o, count in enumerate(out_counts) for k in range(count)]
        for at, ((o, k), options) in enumerate(zip(flat, picks, strict=True)):
            for condition, which, index in options:

                def start(which=which, index=index, o=o, k=k, at=at):
                    pltpu.make_async_copy(src[which].at[index(plan_ref)], outs[o].at[k], sem.at[at]).start()

                pl.when(condition(plan_ref))(start)
        for at, (o, k) in enumerate(flat):
            pltpu.make_async_copy(outs[o].at[k], outs[o].at[k], sem.at[at]).wait()

    return pl.pallas_call(
        kernel,
        out_shape=[jax.ShapeDtypeStruct((count, rows, cols_), BF) for count in out_counts],
        in_specs=[SMEM] + [ANY] * n_src,
        out_specs=[pl.BlockSpec(memory_space=pltpu.VMEM)] * len(out_counts),
        scratch_shapes=[pltpu.SemaphoreType.DMA((len(picks),))],
        compiler_params=pltpu.CompilerParams(vmem_limit_bytes=VMEM_LIMIT),
        name="pick",
    )(plan, *sources)


def slot_kernel(size, cap, g_cands, cands, n_pieces, plan_ref, ours_ref, theirs_ref, mine_ref, other_ref, *refs):
    pieces = refs[:n_pieces]
    left_stat, right_stat, new_left, new_right, out_ref, left, right, grad, raw, sem = refs[n_pieces:]
    step = pl.program_id(0)
    z, core = plan_ref[ZPOS], plan_ref[CORE]
    block, cols = raw.shape
    rows = block // size
    half = rows // 2

    def fetch(s):
        def copy_half(source, shard, side):
            row = pl.multiple_of(shard * rows + side * half, 16)
            pltpu.make_async_copy(source, grad.at[s, pl.ds(row, half), :], sem.at[s, 2]).start()

        def copy_rows(source, shard, held, kind):
            row = pl.multiple_of(shard * rows, 16)
            pltpu.make_async_copy(source, held.at[s, pl.ds(row, rows), :], sem.at[s, kind]).start()

        live = plan_ref[LIVE + s] == 1

        @pl.when(live)
        def _():
            copy_half(ours_ref.at[s], z, core)
            copy_half(theirs_ref.at[s], z, 1 - core)

        for number, local, partner in g_cands:

            @pl.when(jnp.logical_and(live, plan_ref[CAND + s] == number))
            def _():
                for chosen, side in ((local, core), (partner, 1 - core)):
                    for ref, index, row, offset in chosen:
                        copy_half(pieces[ref].at[index, row : row + half], lax.rem(z + offset, size), side)

        for kind, held in ((0, left), (1, right)):
            for here in (True, False):
                use = jnp.logical_and(live, core == kind if here else core != kind)

                @pl.when(use)
                def _():
                    copy_rows((mine_ref if here else other_ref).at[s], z, held, kind)

                for number, local, partner in cands:

                    @pl.when(jnp.logical_and(use, plan_ref[CAND + s] == number))
                    def _():
                        for ref, index, row, offset in local if here else partner:
                            copy_rows(pieces[ref].at[index, row : row + rows], lax.rem(z + offset, size), held, kind)

    @pl.when(step == 0)
    def _():
        for s in range(cap):
            fetch(s)

    live = plan_ref[LIVE + step] == 1
    scale = (1.0 - STAT_DECAY) / cols

    @pl.when(live)
    def _():
        pltpu.make_async_copy(grad.at[step], grad.at[step], sem.at[step, 2]).wait()
        start = pl.multiple_of(z * rows, 128)
        g_rows = grad[step, pl.ds(start, rows), :]
        g_cols = grad[step, :, pl.ds(start, rows)]
        made = lax.dot_general(g_rows, grad[step], (((1,), (1,)), ((), ())), preferred_element_type=F32)
        new_left[0] = STAT_DECAY * left_stat[0] + scale * made
        made = lax.dot_general(g_cols, grad[step], (((0,), (0,)), ((), ())), preferred_element_type=F32)
        new_right[0] = STAT_DECAY * right_stat[0] + scale * made
        for kind, held in ((0, left), (1, right)):
            pltpu.make_async_copy(held.at[step], held.at[step], sem.at[step, kind]).wait()
        g_square = jnp.zeros((8, cols), F32)
        raw_square = jnp.zeros((8, cols), F32)
        tile = 256
        for r in range(0, block, tile):
            part = jnp.dot(left[step, r : r + tile, :], grad[step], preferred_element_type=F32).astype(BF)
            made = jnp.dot(part, right[step], preferred_element_type=F32)
            raw[r : r + tile, :] = made
            raw_square += jnp.sum((made * made).reshape(tile // 8, 8, cols), axis=0)
            g = grad[step, r : r + tile, :].astype(F32)
            g_square += jnp.sum((g * g).reshape(tile // 8, 8, cols), axis=0)
        top = jnp.sum(g_square, axis=(0, 1), keepdims=True) + EPSILON
        bottom = jnp.sum(raw_square, axis=(0, 1), keepdims=True) + EPSILON
        out_ref[0] = (raw[...] * jnp.sqrt(top / bottom)).astype(BF)

    @pl.when(jnp.logical_not(live))
    def _():
        new_left[0] = STAT_DECAY * left_stat[0]
        new_right[0] = STAT_DECAY * right_stat[0]
        out_ref[0] = jnp.zeros_like(out_ref[0])


def step_at(level, spill, plan, core, grads, stat_left, stat_right, inv_left, inv_right):
    size, workers = lax.axis_size("dp"), lax.axis_size("worker")
    z = lax.axis_index("dp")
    cap, rows, cols = inv_left.shape
    block, part = rows * size, rows // 2
    around = [(i, (i + 1) % size) for i in range(size)]
    ring = lambda x: lax.ppermute(x, "dp", around)
    across = lambda x, k: lax.ppermute(x, "worker", [(i, i ^ k) for i in range(workers)])

    def after(given, *xs):
        xs = lax.optimization_barrier((*xs, *given))[: len(xs)]
        return xs if len(xs) > 1 else xs[0]

    numbers = list(range(level)) + ([100, 101] if spill else [])

    def bring(cands, arrays, t, moved, row):
        found = [(moved, u) for u in range(level)]
        if spill:
            found += [(across(moved[0:1], 2), 0), (across(moved[1:2], 4), 0)]
        twins, ends = {}, []
        for (_, local, partner), (array, index) in zip(cands, found, strict=True):
            if id(array) not in twins:
                twins[id(array)] = len(arrays)
                arrays.extend([array, across(array, 1)])
            at = twins[id(array)]
            local.append((at, index, row, size - t))
            partner.append((at + 1, index, row, size - t))
            ends.append((at, index))
        return ends

    g = grads.reshape(size, rows, cols)

    sends = [lax.dynamic_index_in_dim(g, lax.rem(z + k, size), 0, keepdims=False) for k in range(1, size)]
    sends = lax.optimization_barrier(sends)
    arrived = [lax.ppermute(a, "dp", [(i, (i + k) % size) for i in range(size)]) for k, a in enumerate(sends, 1)]
    inv_left, inv_right = after((across(sends[0][:16, :128], 1),), inv_left, inv_right)

    left_b, right_b = inv_left.astype(BF), inv_right.astype(BF)
    mine = jnp.where(core == 0, left_b, right_b)
    other = jnp.where(core == 0, right_b, left_b)
    theirs = across(other, 1)
    seat_of = lambda at: [
        (lambda plan_ref: plan_ref[at] < cap, 0, lambda plan_ref: plan_ref[at]),
        (lambda plan_ref: plan_ref[at] >= cap, 1, lambda plan_ref: plan_ref[at] - cap),
    ]
    sources = [mine, theirs]
    picks = [seat_of(SEAT + i) for i in range(level)]
    if spill:
        out_x, out_y = pick(plan, [seat_of(XSHIP), seat_of(YSHIP)], sources, rows, cols, (1, 1))
        sources += [across(out_x, 2), across(out_y, 4)]
        for i, flag in ((0, XIN), (1, YIN)):
            own_options = [
                (lambda plan_ref, c=c, flag=flag: jnp.logical_and(c(plan_ref), plan_ref[flag] == 0), which, index)
                for c, which, index in picks[i]
            ]
            picks[i] = own_options + [(lambda plan_ref, flag=flag: plan_ref[flag] == 1, 2 + i, lambda plan_ref: 0)]
    (units,) = pick(plan, picks, sources, rows, cols, (level,))
    arrived = after((units,), *arrived)
    root = [ring(after(arrived, units))]
    own = lax.dynamic_index_in_dim(g, z, 0, keepdims=False).astype(F32)
    own = (sum((a.astype(F32) for a in arrived), own) / size).astype(BF)

    halves = own.reshape(2, part, cols)
    keep = lax.dynamic_index_in_dim(halves, core, 0, keepdims=False)
    give = lax.dynamic_index_in_dim(halves, 1 - core, 0, keepdims=False)
    home = jnp.stack([keep, across(give, 1)])
    n_bits = workers.bit_length() - 1
    if n_bits == 3:
        from_x, from_y = across(home, 2), across(home, 4)
        corner = [across(from_x[0:1], 4), across(from_y[1:2], 2)]
        spread = [home, from_x, from_y, *corner]
        where_is = [(0, 0), (0, 1), (1, 0), (1, 1), (2, 0), (2, 1), (3, 0), (4, 0)]
    else:
        spread = [home]
        for b in range(1, n_bits):
            spread += [across(array, 1 << b) for array in spread]
        where_is = [(j >> 1, j & 1) for j in range(workers)]
    block_of = lambda at: [
        (lambda plan_ref, j=j: plan_ref[at] == j, which, lambda plan_ref, index=index: index)
        for j, (which, index) in enumerate(where_is)
    ]
    arrays, cands = [], [(number, [], []) for number in numbers]
    g_cands = [(number, [], []) for number in numbers]
    wanted = [block_of(UNIT + i) for i in range(level)]
    wanted += [block_of(BLOCK + s) for s in range(cap)] + [block_of(MATE + s) for s in range(cap)]
    g_units, g_ours, g_mates = pick(plan, wanted, spread, part, cols, (level, cap, cap))
    g_theirs = across(g_mates, 1)
    packed = jnp.concatenate([root[0], g_units], axis=1)
    bring(cands, arrays, 1, after(spread[1:], root[0]), 0)
    for t in range(1, size):
        packed, start = ring(packed), len(arrays)
        came = packed
        if t == size - 2:
            packed = packed[:, rows:]
            came = after((packed,), came)
        found = bring(cands, arrays, t + 1, came, 0) if t < size - 1 else bring(g_cands, arrays, t, came, 0)
        if t < size - 1:
            for (_, local, partner), (at, index) in zip(g_cands, found, strict=True):
                local.append((at, index, rows, size - t))
                partner.append((at + 1, index, rows, size - t))
            packed, *arrays[:start] = lax.optimization_barrier((packed, *arrays[:start]))

    slot = lambda r: pl.BlockSpec((1, r, cols), lambda s: (s, 0, 0))
    return pl.pallas_call(
        functools.partial(slot_kernel, size, cap, g_cands, cands, len(arrays)),
        grid=(cap,),
        out_shape=[
            jax.ShapeDtypeStruct((cap, rows, cols), F32),
            jax.ShapeDtypeStruct((cap, rows, cols), F32),
            jax.ShapeDtypeStruct((cap, block, cols), BF),
        ],
        in_specs=[SMEM] + [ANY] * (4 + len(arrays)) + [slot(rows), slot(rows)],
        out_specs=[slot(rows), slot(rows), slot(block)],
        scratch_shapes=[pltpu.VMEM((cap, block, cols), BF) for _ in range(3)]
        + [pltpu.VMEM((block, cols), F32), pltpu.SemaphoreType.DMA((cap, 3))],
        compiler_params=pltpu.CompilerParams(vmem_limit_bytes=VMEM_LIMIT),
        name="slots",
    )(plan, g_ours, g_theirs, mine, other, *arrays, stat_left, stat_right)


def on_device(grads, owner_slots, owner_counts, stat_left, stat_right, inv_left, inv_right):
    workers = lax.axis_size("worker")
    cap = owner_slots.shape[1]
    cols = workers // 2
    spill = cols == 4
    where = jnp.stack([lax.axis_index("dp"), lax.axis_index("worker")]).astype(jnp.int32)
    plan = pl.pallas_call(
        functools.partial(plan_kernel, spill, cap, cols),
        out_shape=jax.ShapeDtypeStruct((PLAN,), jnp.int32),
        in_specs=[SMEM] * 3,
        out_specs=SMEM,
        name="plan",
    )(where, owner_slots, owner_counts)
    core = lax.axis_index("worker") % 2
    levels = range(2, 5) if spill else [2 * cap]
    branches = [functools.partial(step_at, level, spill) for level in levels]
    operands = (plan, core, grads[0, 0], stat_left[0], stat_right[0], inv_left[0], inv_right[0])
    if spill:
        outs = lax.switch(plan[LEVEL] - levels[0], branches, *operands)
    else:
        outs = branches[0](*operands)
    return tuple(out[None] for out in outs)


def solution(mesh):
    return jax.shard_map(
        on_device,
        mesh=mesh,
        in_specs=(
            P("dp", "worker", None, None),
            P(),
            P(),
            P("worker", None, "dp", None),
            P("worker", None, "dp", None),
            P("worker", None, "dp", None),
            P("worker", None, "dp", None),
        ),
        out_specs=(
            P("worker", None, "dp", None),
            P("worker", None, "dp", None),
            P("worker", None, None, None),
        ),
        check_vma=False,
    )
```

```python
import functools
import jax
import jax.numpy as jnp
from jax import lax
from jax.experimental import pallas as pl
from jax.experimental.pallas import tpu as pltpu
from jax.sharding import PartitionSpec as P

STAT_DECAY = 0.9
EPSILON = 1e-06
BF = jnp.bfloat16
F32 = jnp.float32
ANY = pl.BlockSpec(memory_space=pl.ANY)
SMEM = pl.BlockSpec(memory_space=pltpu.SMEM)
VMEM_LIMIT = 56 * 1024 * 1024

LEVEL, CORE, ZPOS, XSHIP, YSHIP, XIN, YIN = range(7)
SEAT = 8
LIVE = 16
BLOCK = 20
CAND = 24
MATE = 28
UNIT = 32
PLAN = 40


def plan_kernel(spill, cap, cols, where_ref, slots_ref, counts_ref, out_ref):
    z, w = where_ref[0], where_ref[1]
    core, col = lax.rem(w, 2), lax.div(w, 2)
    per = lambda c: counts_ref[2 * c] + counts_ref[2 * c + 1]
    per_col = [counts_ref[2 * c] + counts_ref[2 * c + 1] for c in range(cols)]
    if spill:
        combo = lax.broadcasted_iota(jnp.int32, (8, 128), 0) * 128 + lax.broadcasted_iota(jnp.int32, (8, 128), 1)
        combo = combo & 255
        bit = [(combo >> k) & 1 for k in range(8)]
        worst = jnp.zeros((8, 128), jnp.int32)
        bad = jnp.zeros((8, 128), jnp.int32)
        ships = jnp.zeros((8, 128), jnp.int32)
        for c in range(4):
            out = bit[c] + bit[4 + c]
            load = per_col[c] - out + bit[c ^ 1] + bit[4 + (c ^ 2)]
            worst = jnp.maximum(worst, load)
            bad = jnp.maximum(bad, jnp.where(out > per_col[c], 1, 0))
            ships = ships + out
        cost = (worst * 16 + ships + bad * 1024) * 256 + combo
        best = jnp.min(cost.astype(F32)).astype(jnp.int32)
        level = lax.div(best, 4096)
        flows = best & 255
        flag = lambda k: (flows >> k) & 1
        xship, yship = flag(col), flag(4 + col)
        xin, yin = flag(col ^ 1), flag(4 + (col ^ 2))
    else:
        level = functools.reduce(jnp.maximum, per_col)
        xship = yship = xin = yin = jnp.int32(0)
    if spill:
        x_rank = per(col ^ 1) - 1
        y_rank = per(col ^ 2) - 1 - flag(col ^ 2)
    first = counts_ref[2 * col]
    mine = counts_ref[2 * col + 1] + first

    def seat(rank):
        c = jnp.where(rank < first, 0, 1)
        s = jnp.minimum(jnp.maximum(rank - c * first, 0), cap - 1)
        return jnp.where(c == core, 0, cap) + s

    def block_at(column, rank):
        start = counts_ref[2 * column]
        c = jnp.where(rank < start, 0, 1)
        return slots_ref[2 * column + c, jnp.minimum(jnp.maximum(rank - c * start, 0), cap - 1)] ^ w

    out_ref[LEVEL] = level
    out_ref[CORE] = core
    out_ref[ZPOS] = z
    out_ref[XIN] = xin
    out_ref[YIN] = yin
    out_ref[XSHIP] = seat(mine - 1)
    out_ref[YSHIP] = seat(mine - 1 - xship)
    for i in range(2 * cap):
        rank = 0 if i == 0 else (1 - xin if i == 1 else i - xin - yin)
        out_ref[SEAT + i] = seat(jnp.int32(rank))
        block = block_at(col, jnp.int32(rank))
        if spill and i == 0:
            block = jnp.where(xin == 1, block_at(col ^ 1, x_rank), block)
        if spill and i == 1:
            block = jnp.where(yin == 1, block_at(col ^ 2, y_rank), block)
        out_ref[UNIT + i] = block
    for s in range(cap):
        rank = s + core * first
        out_ref[LIVE + s] = jnp.where(s < counts_ref[w], 1, 0)
        out_ref[BLOCK + s] = slots_ref[w, s] ^ w
        out_ref[MATE + s] = slots_ref[w ^ 1, s] ^ w
        place = jnp.where(xin + yin == 0, rank, jnp.where(xin == 0, jnp.where(rank == 0, 0, rank + 1), rank + xin + yin))
        sent_x = jnp.logical_and(xship == 1, rank == mine - 1)
        sent_y = jnp.logical_and(yship == 1, rank == mine - 1 - xship)
        out_ref[CAND + s] = jnp.where(sent_x, 100, jnp.where(sent_y, 101, place))


def pick(plan, picks, sources, rows, cols_, out_counts):
    n_src = len(sources)

    def kernel(plan_ref, *refs):
        src, outs, sem = refs[:n_src], refs[n_src:-1], refs[-1]
        flat = [(o, k) for o, count in enumerate(out_counts) for k in range(count)]
        for at, ((o, k), options) in enumerate(zip(flat, picks, strict=True)):
            for condition, which, index in options:

                def start(which=which, index=index, o=o, k=k, at=at):
                    pltpu.make_async_copy(src[which].at[index(plan_ref)], outs[o].at[k], sem.at[at]).start()

                pl.when(condition(plan_ref))(start)
        for at, (o, k) in enumerate(flat):
            pltpu.make_async_copy(outs[o].at[k], outs[o].at[k], sem.at[at]).wait()

    return pl.pallas_call(
        kernel,
        out_shape=[jax.ShapeDtypeStruct((count, rows, cols_), BF) for count in out_counts],
        in_specs=[SMEM] + [ANY] * n_src,
        out_specs=[pl.BlockSpec(memory_space=pltpu.VMEM)] * len(out_counts),
        scratch_shapes=[pltpu.SemaphoreType.DMA((len(picks),))],
        compiler_params=pltpu.CompilerParams(vmem_limit_bytes=VMEM_LIMIT),
        name="pick",
    )(plan, *sources)


def slot_kernel(size, cap, g_cands, cands, n_pieces, plan_ref, ours_ref, theirs_ref, mine_ref, other_ref, *refs):
    pieces = refs[:n_pieces]
    left_stat, right_stat, new_left, new_right, out_ref, left, right, grad, raw, sem = refs[n_pieces:]
    step = pl.program_id(0)
    z, core = plan_ref[ZPOS], plan_ref[CORE]
    block, cols = raw.shape
    rows = block // size
    half = rows // 2

    def fetch(s):
        def copy_half(source, shard, side):
            row = pl.multiple_of(shard * rows + side * half, 16)
            pltpu.make_async_copy(source, grad.at[s, pl.ds(row, half), :], sem.at[s, 2]).start()

        def copy_rows(source, shard, held, kind):
            row = pl.multiple_of(shard * rows, 16)
            pltpu.make_async_copy(source, held.at[s, pl.ds(row, rows), :], sem.at[s, kind]).start()

        live = plan_ref[LIVE + s] == 1

        @pl.when(live)
        def _():
            copy_half(ours_ref.at[s], z, core)
            copy_half(theirs_ref.at[s], z, 1 - core)

        for number, local, partner in g_cands:

            @pl.when(jnp.logical_and(live, plan_ref[CAND + s] == number))
            def _():
                for chosen, side in ((local, core), (partner, 1 - core)):
                    for ref, index, row, offset in chosen:
                        copy_half(pieces[ref].at[index, row : row + half], lax.rem(z + offset, size), side)

        for kind, held in ((0, left), (1, right)):
            for here in (True, False):
                use = jnp.logical_and(live, core == kind if here else core != kind)

                @pl.when(use)
                def _():
                    copy_rows((mine_ref if here else other_ref).at[s], z, held, kind)

                for number, local, partner in cands:

                    @pl.when(jnp.logical_and(use, plan_ref[CAND + s] == number))
                    def _():
                        for ref, index, row, offset in local if here else partner:
                            copy_rows(pieces[ref].at[index, row : row + rows], lax.rem(z + offset, size), held, kind)

    @pl.when(step == 0)
    def _():
        for s in range(cap):
            fetch(s)

    live = plan_ref[LIVE + step] == 1
    scale = (1.0 - STAT_DECAY) / cols

    @pl.when(live)
    def _():
        pltpu.make_async_copy(grad.at[step], grad.at[step], sem.at[step, 2]).wait()
        start = pl.multiple_of(z * rows, 128)
        g_rows = grad[step, pl.ds(start, rows), :]
        g_cols = grad[step, :, pl.ds(start, rows)]
        made = lax.dot_general(g_rows, grad[step], (((1,), (1,)), ((), ())), preferred_element_type=F32)
        new_left[0] = STAT_DECAY * left_stat[0] + scale * made
        made = lax.dot_general(g_cols, grad[step], (((0,), (0,)), ((), ())), preferred_element_type=F32)
        new_right[0] = STAT_DECAY * right_stat[0] + scale * made
        for kind, held in ((0, left), (1, right)):
            pltpu.make_async_copy(held.at[step], held.at[step], sem.at[step, kind]).wait()
        g_square = jnp.zeros((8, cols), F32)
        raw_square = jnp.zeros((8, cols), F32)
        tile = 256
        for r in range(0, block, tile):
            part = jnp.dot(left[step, r : r + tile, :], grad[step], preferred_element_type=F32).astype(BF)
            made = jnp.dot(part, right[step], preferred_element_type=F32)
            raw[r : r + tile, :] = made
            raw_square += jnp.sum((made * made).reshape(tile // 8, 8, cols), axis=0)
            g = grad[step, r : r + tile, :].astype(F32)
            g_square += jnp.sum((g * g).reshape(tile // 8, 8, cols), axis=0)
        top = jnp.sum(g_square, axis=(0, 1), keepdims=True) + EPSILON
        bottom = jnp.sum(raw_square, axis=(0, 1), keepdims=True) + EPSILON
        out_ref[0] = (raw[...] * jnp.sqrt(top / bottom)).astype(BF)

    @pl.when(jnp.logical_not(live))
    def _():
        new_left[0] = STAT_DECAY * left_stat[0]
        new_right[0] = STAT_DECAY * right_stat[0]
        out_ref[0] = jnp.zeros_like(out_ref[0])


def step_at(level, spill, plan, core, grads, stat_left, stat_right, inv_left, inv_right):
    size, workers = lax.axis_size("dp"), lax.axis_size("worker")
    z = lax.axis_index("dp")
    cap, rows, cols = inv_left.shape
    block, part = rows * size, rows // 2
    around = [(i, (i + 1) % size) for i in range(size)]
    ring = lambda x: lax.ppermute(x, "dp", around)
    across = lambda x, k: lax.ppermute(x, "worker", [(i, i ^ k) for i in range(workers)])

    def after(given, *xs):
        xs = lax.optimization_barrier((*xs, *given))[: len(xs)]
        return xs if len(xs) > 1 else xs[0]

    numbers = list(range(level)) + ([100, 101] if spill else [])

    def bring(cands, arrays, t, moved, row):
        found = [(moved, u) for u in range(level)]
        if spill:
            found += [(across(moved[0:1], 2), 0), (across(moved[1:2], 4), 0)]
        twins, ends = {}, []
        for (_, local, partner), (array, index) in zip(cands, found, strict=True):
            if id(array) not in twins:
                twins[id(array)] = len(arrays)
                arrays.extend([array, across(array, 1)])
            at = twins[id(array)]
            local.append((at, index, row, size - t))
            partner.append((at + 1, index, row, size - t))
            ends.append((at, index))
        return ends

    g = grads.reshape(size, rows, cols)

    sends = [lax.dynamic_index_in_dim(g, lax.rem(z + k, size), 0, keepdims=False) for k in range(1, size)]
    sends = lax.optimization_barrier(sends)
    arrived = [lax.ppermute(a, "dp", [(i, (i + k) % size) for i in range(size)]) for k, a in enumerate(sends, 1)]
    inv_left, inv_right = after((across(sends[0][:16, :128], 1),), inv_left, inv_right)

    other = jnp.where(core == 0, inv_right, inv_left).astype(BF)
    other, inv_left, inv_right = lax.optimization_barrier((other, inv_left, inv_right))
    theirs = across(other, 1)
    mine = jnp.where(core == 0, inv_left, inv_right).astype(BF)
    seat_of = lambda at: [
        (lambda plan_ref: plan_ref[at] < cap, 0, lambda plan_ref: plan_ref[at]),
        (lambda plan_ref: plan_ref[at] >= cap, 1, lambda plan_ref: plan_ref[at] - cap),
    ]
    sources = [mine, theirs]
    picks = [seat_of(SEAT + i) for i in range(level)]
    if spill:
        out_x, out_y = pick(plan, [seat_of(XSHIP), seat_of(YSHIP)], sources, rows, cols, (1, 1))
        sources += [across(out_x, 2), across(out_y, 4)]
        for i, flag in ((0, XIN), (1, YIN)):
            own_options = [
                (lambda plan_ref, c=c, flag=flag: jnp.logical_and(c(plan_ref), plan_ref[flag] == 0), which, index)
                for c, which, index in picks[i]
            ]
            picks[i] = own_options + [(lambda plan_ref, flag=flag: plan_ref[flag] == 1, 2 + i, lambda plan_ref: 0)]
    (units,) = pick(plan, picks, sources, rows, cols, (level,))
    arrived = after((units,), *arrived)
    root = [ring(after(arrived, units))]
    own = lax.dynamic_index_in_dim(g, z, 0, keepdims=False).astype(F32)
    own = (sum((a.astype(F32) for a in arrived), own) / size).astype(BF)

    halves = own.reshape(2, part, cols)
    keep = lax.dynamic_index_in_dim(halves, core, 0, keepdims=False)
    give = lax.dynamic_index_in_dim(halves, 1 - core, 0, keepdims=False)
    home = jnp.stack([keep, across(give, 1)])
    n_bits = workers.bit_length() - 1
    if n_bits == 3:
        from_x, from_y = across(home, 2), across(home, 4)
        corner = [across(from_x[0:1], 4), across(from_y[1:2], 2)]
        spread = [home, from_x, from_y, *corner]
        where_is = [(0, 0), (0, 1), (1, 0), (1, 1), (2, 0), (2, 1), (3, 0), (4, 0)]
    else:
        spread = [home]
        for b in range(1, n_bits):
            spread += [across(array, 1 << b) for array in spread]
        where_is = [(j >> 1, j & 1) for j in range(workers)]
    block_of = lambda at: [
        (lambda plan_ref, j=j: plan_ref[at] == j, which, lambda plan_ref, index=index: index)
        for j, (which, index) in enumerate(where_is)
    ]
    arrays, cands = [], [(number, [], []) for number in numbers]
    g_cands = [(number, [], []) for number in numbers]
    wanted = [block_of(UNIT + i) for i in range(level)]
    wanted += [block_of(BLOCK + s) for s in range(cap)] + [block_of(MATE + s) for s in range(cap)]
    g_units, g_ours, g_mates = pick(plan, wanted, spread, part, cols, (level, cap, cap))
    g_theirs = across(g_mates, 1)
    packed = jnp.concatenate([root[0], g_units], axis=1)
    bring(cands, arrays, 1, after(spread[1:], root[0]), 0)
    for t in range(1, size):
        packed, start = ring(packed), len(arrays)
        came = packed
        if t == size - 2:
            packed = packed[:, rows:]
            came = after((packed,), came)
        found = bring(cands, arrays, t + 1, came, 0) if t < size - 1 else bring(g_cands, arrays, t, came, 0)
        if t < size - 1:
            for (_, local, partner), (at, index) in zip(g_cands, found, strict=True):
                local.append((at, index, rows, size - t))
                partner.append((at + 1, index, rows, size - t))
            packed, *arrays[:start] = lax.optimization_barrier((packed, *arrays[:start]))

    slot = lambda r: pl.BlockSpec((1, r, cols), lambda s: (s, 0, 0))
    return pl.pallas_call(
        functools.partial(slot_kernel, size, cap, g_cands, cands, len(arrays)),
        grid=(cap,),
        out_shape=[
            jax.ShapeDtypeStruct((cap, rows, cols), F32),
            jax.ShapeDtypeStruct((cap, rows, cols), F32),
            jax.ShapeDtypeStruct((cap, block, cols), BF),
        ],
        in_specs=[SMEM] + [ANY] * (4 + len(arrays)) + [slot(rows), slot(rows)],
        out_specs=[slot(rows), slot(rows), slot(block)],
        scratch_shapes=[pltpu.VMEM((cap, block, cols), BF) for _ in range(3)]
        + [pltpu.VMEM((block, cols), F32), pltpu.SemaphoreType.DMA((cap, 3))],
        compiler_params=pltpu.CompilerParams(vmem_limit_bytes=VMEM_LIMIT),
        name="slots",
    )(plan, g_ours, g_theirs, mine, other, *arrays, stat_left, stat_right)


def on_device(grads, owner_slots, owner_counts, stat_left, stat_right, inv_left, inv_right):
    workers = lax.axis_size("worker")
    cap = owner_slots.shape[1]
    cols = workers // 2
    spill = cols == 4
    where = jnp.stack([lax.axis_index("dp"), lax.axis_index("worker")]).astype(jnp.int32)
    plan = pl.pallas_call(
        functools.partial(plan_kernel, spill, cap, cols),
        out_shape=jax.ShapeDtypeStruct((PLAN,), jnp.int32),
        in_specs=[SMEM] * 3,
        out_specs=SMEM,
        name="plan",
    )(where, owner_slots, owner_counts)
    core = lax.axis_index("worker") % 2
    levels = range(2, 5) if spill else [2 * cap]
    branches = [functools.partial(step_at, level, spill) for level in levels]
    operands = (plan, core, grads[0, 0], stat_left[0], stat_right[0], inv_left[0], inv_right[0])
    if spill:
        outs = lax.switch(plan[LEVEL] - levels[0], branches, *operands)
    else:
        outs = branches[0](*operands)
    return tuple(out[None] for out in outs)


def solution(mesh):
    return jax.shard_map(
        on_device,
        mesh=mesh,
        in_specs=(
            P("dp", "worker", None, None),
            P(),
            P(),
            P("worker", None, "dp", None),
            P("worker", None, "dp", None),
            P("worker", None, "dp", None),
            P("worker", None, "dp", None),
        ),
        out_specs=(
            P("worker", None, "dp", None),
            P("worker", None, "dp", None),
            P("worker", None, None, None),
        ),
        check_vma=False,
    )
```
